32 devices in a mesh: grp: 2 (over x), exp: 8 (over z, y), sp: 2 (over core).
Axes of the slice: x: 2, y: 2, z: 4, core: 2. Of those that a mesh axis runs over, the one named last changes fastest.
Arguments:
- tokens: bfloat16 [2048, 2560], P(('grp', 'exp')), parts along dimension 0, may hold values from -6 to 6
- cotangent: bfloat16 [2048, 2560], P(('grp', 'exp')), parts along dimension 0, may hold values from -0.59765625 to 0.59765625
- expert_ids: int32 [2048, 6], P(('grp', 'exp')), parts along dimension 0, may hold values from 0 to 7, as said below
- slot_ids: int32 [2048, 6], P(('grp', 'exp')), parts along dimension 0, may hold values from 0 to 119, as said below
- gates: float32 [2048, 6], P(('grp', 'exp')), parts along dimension 0, may hold values from 0.1 to 4
- w_gate: bfloat16 [8, 2560, 768], P('exp', None, 'sp'), may hold values from -0.125 to 0.125
- w_up: bfloat16 [8, 2560, 768], P('exp', None, 'sp'), may hold values from -0.125 to 0.125
- w_down: bfloat16 [8, 2560, 768], P('exp', None, 'sp'), may hold values from -0.21875 to 0.21875
- s_gate: bfloat16 [2560, 1536], P('exp', 'sp'), may hold values from -0.125 to 0.125
- s_up: bfloat16 [2560, 1536], P('exp', 'sp'), may hold values from -0.125 to 0.125
- s_down: bfloat16 [2560, 1536], P('exp', 'sp'), may hold values from -0.15625 to 0.15625
Outputs:
- input_grad: bfloat16 [2048, 2560], P(('grp', 'exp'), 'sp'), parts along dimension 0
- gate_grads: float32 [2048, 6], P(('grp', 'exp'), 'sp'), parts along dimension 0
The draws below stay inside these ranges and needn't reach their ends.
There are 2 independent parts, one for each index of `grp`. The reference program is written for one: setup_inputs(seed, part) draws one part's arguments, and reference() takes and returns one part's arrays. A program takes and returns all parts, laid end to end along the dimension named above; an argument that names none is the same for every part. Nothing has to cross between parts.
Inputs may be any that keep to these rules, and one draw needn't show every extreme that they name: `expert_ids`: each row names 6 different experts. In each aligned block of 128 rows (the rows of one index of exp) no expert is named by more than 120 rows; in every block one expert, the same in all blocks of a group, and one more are named by exactly 120 rows, and every expert by at least one. `slot_ids`: within each aligned block of 128 rows, the rows that name one expert hold the slots 0 to their count - 1 for it, each once.
All inputs are finite; a program needn't handle non-finite values.
Results may differ from the reference program's by a relative error of at most 0.0057.
Values may be sent and summed in bfloat16 or wider, within the bound.
A program may use at most 128 MiB of HBM per device.

```python
import math
import jax
import jax.numpy as jnp
from jax import lax

D = 2560
H = 768
SH = 1536
TOP = 6
TOK_DEV = 128
EXPERTS = 8
TOKENS = 1024
CAP = 120
N_SP = 2


def route_tables(key):
    total = TOK_DEV * TOP
    first = jax.random.randint(jax.random.fold_in(key, 11), (), 0, EXPERTS)
    labels = jnp.arange(EXPERTS, dtype=jnp.int32)
    position = jnp.arange(total, dtype=jnp.int32)

    def one_block(block):
        block_key = jax.random.fold_in(key, 100 + block)
        keys = jax.random.split(block_key, 4)
        second = (first + 1 + jax.random.randint(keys[0], (), 0, EXPERTS - 1)) % EXPERTS
        remain = total - 2 * CAP
        base_count = remain // (EXPERTS - 2)
        extra = remain % (EXPERTS - 2)
        order = jax.random.permutation(keys[1], EXPERTS).astype(jnp.int32)
        is_hot = (labels == first) | (labels == second)
        smaller = (order[None, :] < order[:, None]) & jnp.logical_not(is_hot)[None, :]
        rank_other = jnp.sum(smaller.astype(jnp.int32), axis=1)
        counts = jnp.where(is_hot, CAP, base_count + (rank_other < extra).astype(jnp.int32)).astype(jnp.int32)
        starts = jnp.cumsum(counts) - counts
        which = jnp.sum((starts[None, :] <= position[:, None]).astype(jnp.int32), axis=1) - 1
        offset = jax.random.randint(keys[2], (EXPERTS,), 0, CAP)
        within = position - starts[which]
        slot = (within + offset[which]) % counts[which]
        shuffle = jax.random.permutation(keys[3], TOK_DEV).astype(jnp.int32)
        token = shuffle[position % TOK_DEV]
        column = position // TOK_DEV
        ids = jnp.zeros((TOK_DEV, TOP), jnp.int32).at[token, column].set(which)
        slots = jnp.zeros((TOK_DEV, TOP), jnp.int32).at[token, column].set(slot)
        return (ids, slots)
    ids, slots = jax.vmap(one_block)(jnp.arange(TOKENS // TOK_DEV, dtype=jnp.int32))
    return (ids.reshape(TOKENS, TOP), slots.reshape(TOKENS, TOP))


def draw_expert_ids(key, part):
    return route_tables(key)[0]


def draw_slot_ids(key, part):
    return route_tables(key)[1]


def block_scale(rng, extent, cuts, smallest, high):
    gain = 1.0
    for axis_at, shards_of in cuts:
        heights = jax.random.uniform(jax.random.fold_in(jax.random.fold_in(rng, 6), axis_at), (shards_of,), jnp.float32, smallest / len(cuts), high / len(cuts))
        gain = gain * jnp.repeat(jnp.exp(heights), extent[axis_at] // shards_of).reshape((-1,) + (1,) * (len(extent) - 1 - axis_at))
    return gain


def gaussian(key, shape, spread, limit, cuts=(), held_as=jnp.bfloat16):
    level = block_scale(key, shape, cuts, -0.22, 0.18) if cuts else 1.0
    values = jax.random.normal(key, shape, jnp.float32) * spread * level
    return jnp.minimum(jnp.maximum(values, -limit), limit).astype(held_as)


def setup_inputs(seed: int = 0, part: int = 0) -> dict:
    arg_keys = jax.random.split(jax.random.key(seed), 12)
    part_keys = jax.random.split(jax.random.fold_in(arg_keys[11], part), 12)
    return {
        "tokens": gaussian(part_keys[0], (TOKENS, D), 1.0, 6.0, ((0, 8),)),
        "cotangent": gaussian(part_keys[1], (TOKENS, D), 0.1, 0.59765625, ((0, 8),)),
        "expert_ids": draw_expert_ids(jax.random.fold_in(jax.random.fold_in(arg_keys[11], part), 71), part),
        "slot_ids": draw_slot_ids(jax.random.fold_in(jax.random.fold_in(arg_keys[11], part), 71), part),
        "gates": jnp.clip(jnp.exp(math.log(4.0) - 3.6888794 * jax.random.uniform(part_keys[4], (TOKENS, TOP), jnp.float32) ** block_scale(part_keys[4], (TOKENS, TOP), ((0, 8),), -0.2, 0.2)), 0.1, 4.0),
        "w_gate": gaussian(arg_keys[5], (EXPERTS, D, H), D ** -0.5, 0.125, ((0, 8), (2, 2))),
        "w_up": gaussian(arg_keys[6], (EXPERTS, D, H), D ** -0.5, 0.125, ((0, 8), (2, 2))),
        "w_down": gaussian(arg_keys[7], (EXPERTS, D, H), H ** -0.5, 0.21875, ((0, 8), (2, 2))),
        "s_gate": gaussian(arg_keys[8], (D, SH), D ** -0.5, 0.125, ((0, 8), (1, 2))),
        "s_up": gaussian(arg_keys[9], (D, SH), D ** -0.5, 0.125, ((0, 8), (1, 2))),
        "s_down": gaussian(arg_keys[10], (D, SH), SH ** -0.5, 0.15625, ((0, 8), (1, 2))),
    }


def swiglu_grads(gate_pre, up_pre, grad_out):
    sigmoid_val = jax.nn.sigmoid(gate_pre)
    silu_val = gate_pre * sigmoid_val
    grad_gate = grad_out * up_pre * sigmoid_val * (1.0 + gate_pre * (1.0 - sigmoid_val))
    grad_up = grad_out * silu_val
    return grad_gate.astype(jnp.bfloat16), grad_up.astype(jnp.bfloat16), silu_val * up_pre


def contract_back(grads, weight):
    return lax.dot_general(grads, weight, (((1,), (1,)), ((), ())), preferred_element_type=jnp.float32)


def reference(tokens, cotangent, expert_ids, slot_ids, gates, w_gate, w_up, w_down, s_gate, s_up, s_down):
    blocks = TOKENS // TOK_DEV
    flat_index = (expert_ids * CAP + slot_ids).reshape(blocks, TOK_DEV * TOP)
    token_number = jnp.broadcast_to(jnp.arange(TOKENS, dtype=jnp.int32)[:, None], (TOKENS, TOP)).reshape(blocks, TOK_DEV * TOP)
    column_number = jnp.broadcast_to(jnp.arange(TOP, dtype=jnp.int32)[None, :], (TOKENS, TOP)).reshape(blocks, TOK_DEV * TOP)
    block_number = jnp.arange(blocks, dtype=jnp.int32)[:, None]
    slot_owner = jnp.zeros((blocks, EXPERTS * CAP), jnp.int32).at[block_number, flat_index].set(token_number)
    slot_column = jnp.zeros((blocks, EXPERTS * CAP), jnp.int32).at[block_number, flat_index].set(column_number)
    slot_used = jnp.zeros((blocks, EXPERTS * CAP), jnp.float32).at[block_number, flat_index].set(1.0)

    def by_expert(values):
        return jnp.swapaxes(values.reshape(blocks, EXPERTS, CAP), 0, 1).reshape(EXPERTS, blocks * CAP)

    group_units = H // N_SP

    def one_expert(carry, inputs):
        dx_acc, gate_acc = carry
        owner_e, column_e, used_e, gate_w, up_w, down_w = inputs
        rows_x = tokens[owner_e]
        rows_dy = cotangent[owner_e]
        piece_sum = jnp.zeros((rows_x.shape[0], D), jnp.float32)
        gate_sum = jnp.zeros((rows_x.shape[0],), jnp.float32)
        for group in range(N_SP):
            lower = group * group_units
            upper = lower + group_units
            gate_pre = jnp.dot(rows_x, gate_w[:, lower:upper], preferred_element_type=jnp.float32)
            up_pre = jnp.dot(rows_x, up_w[:, lower:upper], preferred_element_type=jnp.float32)
            grad_out = jnp.dot(rows_dy, down_w[:, lower:upper], preferred_element_type=jnp.float32)
            grad_gate, grad_up, hidden = swiglu_grads(gate_pre, up_pre, grad_out)
            part_gate = jnp.sum(grad_out * hidden, axis=1).astype(jnp.bfloat16)
            pieces = (contract_back(grad_gate, gate_w[:, lower:upper]) + contract_back(grad_up, up_w[:, lower:upper])).astype(jnp.bfloat16)
            piece_sum = piece_sum + pieces.astype(jnp.float32)
            gate_sum = gate_sum + part_gate.astype(jnp.float32)
        factor = gates[owner_e, column_e] * used_e
        dx_acc = dx_acc.at[owner_e].add(factor[:, None] * piece_sum)
        gate_acc = gate_acc.at[owner_e, column_e].add(used_e * gate_sum)
        return (dx_acc, gate_acc), None

    start = (jnp.zeros((TOKENS, D), jnp.float32), jnp.zeros((TOKENS, TOP), jnp.float32))
    inputs = (by_expert(slot_owner), by_expert(slot_column), by_expert(slot_used), w_gate, w_up, w_down)
    (dx_acc, gate_acc), unused = lax.scan(one_expert, start, inputs)

    gate_pre = jnp.dot(tokens, s_gate, preferred_element_type=jnp.float32)
    up_pre = jnp.dot(tokens, s_up, preferred_element_type=jnp.float32)
    grad_out = jnp.dot(cotangent, s_down, preferred_element_type=jnp.float32)
    grad_gate, grad_up, hidden = swiglu_grads(gate_pre, up_pre, grad_out)
    shared_dx = contract_back(grad_gate, s_gate) + contract_back(grad_up, s_up)
    input_grad = (dx_acc + shared_dx).astype(jnp.bfloat16)
    return input_grad, gate_acc
```

```python
import functools
import jax
import jax.numpy as jnp
from jax import lax
from jax.experimental import pallas as pl
from jax.experimental.pallas import tpu as pltpu
from jax.sharding import PartitionSpec as P

MESH = pl.DeviceIdType.MESH
LANE = 128


def ceil_lanes(count):
    return (count + LANE - 1) // LANE * LANE


def kernel(
    n, x_ref, dy_ref, ids_ref, gates_ref, wg_ref, wu_ref, wd_ref, shared_ref,
    out_ref, gg_ref,
    tok, weights, pair_out, pair_in, sum_out, sum_in,
    local_sem, tok_send, tok_recv, sib_send, sib_recv, pair_send, pair_recv,
    sum_send, sum_recv, w_send, w_recv, fw_send, fw_recv,
):
    rows, depth = x_ref.shape
    units = wg_ref.shape[2]
    top = ids_ref.shape[1]
    shared_rows = shared_ref.shape[1]
    part_rows = shared_rows // 2
    swide = shared_ref.shape[2] // 3
    half = depth // 2
    half_rows = rows // 2
    x_wide = 2 * units + 2 * swide
    shared_at = 2 * units
    down_at = x_wide
    grp, exp, core = lax.axis_index("grp"), lax.axis_index("exp"), lax.axis_index("sp")
    other_grp, other_core = 1 - grp, 1 - core

    side, along = exp % 2, exp // 2
    place = (1 - side) * along + side * (n - 1 - along)

    def device_at(where):
        back = where // (n // 2)
        return (1 - back) * (2 * where) + back * (2 * (n - 1 - where) + 1)

    onward = (device_at((place + 1) % n), device_at((place + n - 1) % n))

    loads = [
        (x_ref, tok.at[0, 0, :, pl.ds(0, depth)]),
        (dy_ref, tok.at[0, 1, :, pl.ds(0, depth)]),
        (wg_ref.at[0], weights.at[:, pl.ds(0, units)]),
        (wu_ref.at[0], weights.at[:, pl.ds(units, units)]),
        (wd_ref.at[0], weights.at[:, pl.ds(down_at + swide, units)]),
        (
            shared_ref.at[exp],
            weights.at[pl.ds(exp * shared_rows, shared_rows), pl.ds(shared_at, 3 * swide)],
        ),
    ]
    loads = [
        pltpu.make_async_copy(src, dst, local_sem.at[i]) for i, (src, dst) in enumerate(loads)
    ]
    for load in loads:
        load.start()

    barrier = pltpu.get_barrier_semaphore()
    for k in range(1, n):
        pl.semaphore_signal(
            barrier, inc=1, device_id={"exp": (exp + k) % n}, device_id_type=MESH
        )
    pl.semaphore_signal(barrier, inc=1, device_id={"sp": other_core}, device_id_type=MESH)
    pl.semaphore_signal(barrier, inc=1, device_id={"grp": other_grp}, device_id_type=MESH)

    lane = lax.broadcasted_iota(jnp.int32, (rows, LANE), 1)
    factor = jnp.zeros((rows, LANE), jnp.float32)
    for k in range(top):
        hit = (lane % n == ids_ref[:, k : k + 1]) & (lane < 3 * n)
        factor = factor + jnp.where(hit, gates_ref[:, k : k + 1], 0.0)
    first = factor.astype(jnp.bfloat16).astype(jnp.float32)
    second = (factor - first).astype(jnp.bfloat16).astype(jnp.float32)
    third = factor - first - second
    terms = jnp.where(lane < n, first, jnp.where(lane < 2 * n, second, third))
    tok[0, 0, :, pl.ds(depth, LANE)] = terms.astype(jnp.bfloat16)
    tok[0, 1, :, pl.ds(depth, LANE)] = jnp.zeros((rows, LANE), jnp.bfloat16)

    loads[0].wait()
    loads[1].wait()
    pl.semaphore_wait(barrier, n + 1)

    def token_copy(step, way):
        part = pl.ds(way * half_rows, half_rows)
        return pltpu.make_async_remote_copy(
            src_ref=tok.at[step, core, part],
            dst_ref=tok.at[step + 1, core, part],
            send_sem=tok_send.at[way, step],
            recv_sem=tok_recv.at[way, step + 1],
            device_id={"exp": onward[way]},
            device_id_type=MESH,
        )

    def token_arrival(step, way):
        part = pl.ds(way * half_rows, half_rows)
        return pltpu.make_async_remote_copy(
            src_ref=tok.at[step, core, part],
            dst_ref=tok.at[step, core, part],
            send_sem=tok_send.at[way, step],
            recv_sem=tok_recv.at[way, step],
            device_id={"exp": onward[way]},
            device_id_type=MESH,
        )

    def sibling_copy(step, which):
        return pltpu.make_async_remote_copy(
            src_ref=tok.at[step, which],
            dst_ref=tok.at[step, which],
            send_sem=sib_send.at[step],
            recv_sem=sib_recv.at[step],
            device_id={"sp": other_core},
            device_id_type=MESH,
        )

    def pair_copy(step):
        return pltpu.make_async_remote_copy(
            src_ref=pair_out.at[step],
            dst_ref=pair_in.at[step],
            send_sem=pair_send.at[step],
            recv_sem=pair_recv.at[step],
            device_id={"sp": other_core},
            device_id_type=MESH,
        )

    def sum_copy(step, way):
        part = pl.ds(way * half_rows, half_rows)
        return pltpu.make_async_remote_copy(
            src_ref=sum_out.at[step, part],
            dst_ref=sum_in.at[step, part],
            send_sem=sum_send.at[way, step],
            recv_sem=sum_recv.at[way, step],
            device_id={"exp": onward[way]},
            device_id_type=MESH,
        )

    def shared_block(owner, part):
        return weights.at[
            pl.ds(owner * shared_rows + part * part_rows, part_rows),
            pl.ds(shared_at, 3 * swide),
        ]

    def weight_copy(k):
        target = (exp + k) % n
        return pltpu.make_async_remote_copy(
            src_ref=shared_ref.at[target, pl.ds(grp * part_rows, part_rows)],
            dst_ref=shared_block(exp, grp),
            send_sem=w_send.at[k],
            recv_sem=w_recv.at[k],
            device_id={"exp": target},
            device_id_type=MESH,
        )

    def weight_arrival(k):
        block = shared_block((exp + n - k) % n, grp)
        return pltpu.make_async_remote_copy(
            src_ref=block,
            dst_ref=block,
            send_sem=w_send.at[k],
            recv_sem=w_recv.at[k],
            device_id={"exp": (exp + k) % n},
            device_id_type=MESH,
        )

    def weight_forward(k, part):
        block = shared_block((exp + n - k) % n, part)
        return pltpu.make_async_remote_copy(
            src_ref=block,
            dst_ref=block,
            send_sem=fw_send.at[k],
            recv_sem=fw_recv.at[k],
            device_id={"grp": other_grp},
            device_id_type=MESH,
        )

    for way in range(2):
        token_copy(0, way).start()
    for k in range(1, n):
        weight_copy(k).start()

    def back(grads, start, first_unit, unit_count):
        return lax.dot_general(
            grads,
            weights[pl.ds(start, half), pl.ds(first_unit, unit_count)],
            (((1,), (1,)), ((), ())),
            preferred_element_type=jnp.float32,
        )

    def grads_of(gate_pre, up_pre, grad_out):
        sigmoid_val = jax.nn.sigmoid(gate_pre)
        silu_val = gate_pre * sigmoid_val
        grad_gate = grad_out * up_pre * sigmoid_val * (1.0 + gate_pre * (1.0 - sigmoid_val))
        grad_up = grad_out * silu_val
        return (
            jnp.concatenate(
                [grad_gate.astype(jnp.bfloat16), grad_up.astype(jnp.bfloat16)], axis=1
            ),
            silu_val * up_pre,
        )

    def contribution(step):
        forward = jnp.dot(
            tok[step, 0, :, pl.ds(0, depth)],
            weights[:, pl.ds(0, x_wide)],
            preferred_element_type=jnp.float32,
        )
        down = jnp.dot(
            tok[step, 1, :, pl.ds(0, depth)],
            weights[:, pl.ds(down_at, swide + units)],
            preferred_element_type=jnp.float32,
        )
        grad_out = down[:, swide:]
        routed, hidden = grads_of(forward[:, :units], forward[:, units : 2 * units], grad_out)
        shared, unused = grads_of(
            forward[:, shared_at : shared_at + swide],
            forward[:, shared_at + swide :],
            down[:, :swide],
        )
        gate_part = jnp.sum(grad_out * hidden, axis=1, keepdims=True)
        gate_part = gate_part.astype(jnp.bfloat16).astype(jnp.float32)
        terms = tok[step, 0, :, pl.ds(depth, LANE)].astype(jnp.float32)
        mine = (lane % n == exp) & (lane < 3 * n)
        scale = jnp.sum(jnp.where(mine, terms, 0.0), axis=1, keepdims=True)

        def columns(start):
            return scale * back(routed, start, 0, 2 * units) + back(
                shared, start, shared_at, 2 * swide
            )

        extra = jnp.where(lane == exp + n * core, gate_part, 0.0)
        pair_out[step, :, pl.ds(0, half)] = columns(other_core * half)
        pair_out[step, :, pl.ds(half, LANE)] = extra
        pair_copy(step).start()
        return columns(core * half), extra

    def one_step(step, carry):
        for way in range(2):
            token_arrival(step, way).wait_recv()

        @pl.when(step < n - 1)
        def _():
            for way in range(2):
                token_copy(step, way).start()

        sibling_copy(step, core).start()

        @pl.when(step == 1)
        def _():
            for k in range(1, n):
                weight_arrival(k).wait_recv()
                weight_forward(k, grp).start()
            for load in loads[2:]:
                load.wait()
            for k in range(1, n):
                weight_forward(k, other_grp).wait_recv()

        sibling_copy(step, other_core).wait_recv()
        kept, extra = contribution(step)
        pair_copy(step).wait_recv()
        wide = pl.ds(0, half)
        tail = pl.ds(half, LANE)
        kept = kept + pair_in[step, :, wide]
        extra = extra + pair_in[step, :, tail]

        @pl.when(step == 1)
        def _():
            sum_out[step, :, wide] = kept.astype(jnp.bfloat16)
            sum_out[step, :, tail] = extra.astype(jnp.bfloat16)

        @pl.when(step > 1)
        def _():
            for way in range(2):
                sum_copy(step - 1, way).wait_recv()
            total = kept + sum_in[step - 1, :, wide].astype(jnp.float32)
            sum_out[step, :, wide] = total.astype(jnp.bfloat16)
            total = extra + sum_in[step - 1, :, tail].astype(jnp.float32)
            sum_out[step, :, tail] = total.astype(jnp.bfloat16)

        for way in range(2):
            sum_copy(step, way).start()
        return carry

    lax.fori_loop(1, n, one_step, 0)

    kept, extra = contribution(0)
    pair_copy(0).wait_recv()
    for way in range(2):
        sum_copy(n - 1, way).wait_recv()
    wide = pl.ds(0, half)
    tail = pl.ds(half, LANE)
    total = kept + pair_in[0, :, wide] + sum_in[n - 1, :, wide].astype(jnp.float32)
    out_ref[...] = total.astype(jnp.bfloat16)
    extra = extra + pair_in[0, :, tail] + sum_in[n - 1, :, tail].astype(jnp.float32)
    for k in range(top // 2):
        wanted = jnp.where(core == 0, ids_ref[:, k : k + 1], ids_ref[:, k + top // 2 : k + top // 2 + 1])
        hit = (lane % n == wanted) & (lane < 2 * n)
        gg_ref[:, k : k + 1] = jnp.sum(jnp.where(hit, extra, 0.0), axis=1, keepdims=True)

    for k in range(1, n):
        weight_copy(k).wait_send()
        weight_forward(k, grp).wait_send()
    pair_copy(0).wait_send()
    for way in range(2):
        token_copy(0, way).wait_send()

    def drain(step, carry):
        @pl.when(step < n - 1)
        def _():
            for way in range(2):
                token_copy(step, way).wait_send()

        sibling_copy(step, core).wait_send()
        pair_copy(step).wait_send()
        for way in range(2):
            sum_copy(step, way).wait_send()
        return carry

    lax.fori_loop(1, n, drain, 0)


def pack_shared(weight, n):
    row_count, unit_count = weight.shape
    share = unit_count // n
    blocks = jnp.swapaxes(weight.reshape(row_count, n, share), 0, 1)
    return jnp.pad(blocks, ((0, 0), (0, 0), (0, ceil_lanes(share) - share)))


def fused_body(
    tokens, cotangent, expert_ids, slot_ids, gates, w_gate, w_up, w_down, s_gate, s_up, s_down
):
    del slot_ids
    n = lax.axis_size("exp")
    rows, depth = tokens.shape
    units = w_gate.shape[2]
    top = expert_ids.shape[1]
    shared = jnp.concatenate([pack_shared(w, n) for w in (s_gate, s_up, s_down)], axis=2)
    swide = shared.shape[2] // 3
    half = depth // 2
    anywhere = pl.BlockSpec(memory_space=pl.ANY)
    vmem = pl.BlockSpec(memory_space=pltpu.VMEM)
    dma = pltpu.SemaphoreType.DMA
    flops = 2 * n * rows * depth * 5 * (units + swide)
    return pl.pallas_call(
        functools.partial(kernel, n),
        out_shape=(
            jax.ShapeDtypeStruct((rows, half), jnp.bfloat16),
            jax.ShapeDtypeStruct((rows, top // 2), jnp.float32),
        ),
        in_specs=[anywhere, anywhere, vmem, vmem] + [anywhere] * 4,
        out_specs=(vmem, vmem),
        scratch_shapes=[
            pltpu.VMEM((n, 2, rows, depth + LANE), jnp.bfloat16),
            pltpu.VMEM((depth, 3 * units + 3 * swide), jnp.bfloat16),
            pltpu.VMEM((n, rows, half + LANE), jnp.float32),
            pltpu.VMEM((n, rows, half + LANE), jnp.float32),
            pltpu.VMEM((n, rows, half + LANE), jnp.bfloat16),
            pltpu.VMEM((n, rows, half + LANE), jnp.bfloat16),
            dma((6,)),
            dma((2, n)), dma((2, n)),
            dma((n,)), dma((n,)),
            dma((n,)), dma((n,)),
            dma((2, n)), dma((2, n)),
            dma((n,)), dma((n,)),
            dma((n,)), dma((n,)),
        ],
        compiler_params=pltpu.CompilerParams(
            collective_id=0, has_side_effects=True, vmem_limit_bytes=56 * 1024 * 1024
        ),
        cost_estimate=pl.CostEstimate(
            flops=flops, bytes_accessed=32 * 1024 * 1024, transcendentals=0
        ),
    )(tokens, cotangent, expert_ids, gates, w_gate, w_up, w_down, shared)


def swiglu_grads(gate_pre, up_pre, grad_out):
    sigmoid_val = jax.nn.sigmoid(gate_pre)
    silu_val = gate_pre * sigmoid_val
    grad_gate = grad_out * up_pre * sigmoid_val * (1.0 + gate_pre * (1.0 - sigmoid_val))
    grad_up = grad_out * silu_val
    return (grad_gate.astype(jnp.bfloat16), grad_up.astype(jnp.bfloat16), silu_val * up_pre)


def contract_back(grads, weight):
    return lax.dot_general(
        grads, weight, (((1,), (1,)), ((), ())), preferred_element_type=jnp.float32
    )


def run_experts(arrived_x, arrived_dy, w_gate, w_up, w_down):
    local_count = w_gate.shape[0]
    slot_count = arrived_x.shape[1]
    source_count = arrived_x.shape[0] // local_count

    def regroup(values):
        shaped = values.reshape((source_count, local_count) + values.shape[1:])
        return jnp.swapaxes(shaped, 0, 1).reshape(
            (local_count, source_count * slot_count) + values.shape[2:]
        )

    def ungroup(values):
        shaped = values.reshape((local_count, source_count, slot_count) + values.shape[2:])
        return jnp.swapaxes(shaped, 0, 1).reshape(
            (source_count * local_count, slot_count) + values.shape[2:]
        )

    rows_x = regroup(arrived_x)
    rows_dy = regroup(arrived_dy)
    gate_pre = jnp.einsum("erd,edh->erh", rows_x, w_gate, preferred_element_type=jnp.float32)
    up_pre = jnp.einsum("erd,edh->erh", rows_x, w_up, preferred_element_type=jnp.float32)
    grad_out = jnp.einsum("erd,edh->erh", rows_dy, w_down, preferred_element_type=jnp.float32)
    grad_gate, grad_up, hidden = swiglu_grads(gate_pre, up_pre, grad_out)
    part_gate = jnp.sum(grad_out * hidden, axis=2).astype(jnp.bfloat16)
    both_grads = jnp.concatenate([grad_gate, grad_up], axis=2)
    both_weights = jnp.concatenate([w_gate, w_up], axis=2)
    pieces = jnp.einsum(
        "erh,edh->erd", both_grads, both_weights, preferred_element_type=jnp.float32
    )
    return (ungroup(pieces.astype(jnp.bfloat16)), ungroup(part_gate))


def body(
    tokens, cotangent, expert_ids, slot_ids, gates, w_gate, w_up, w_down, s_gate, s_up, s_down
):
    row_count, feature_count = tokens.shape
    top_count = expert_ids.shape[1]
    experts = w_gate.shape[0] * lax.axis_size("exp")
    capacity = min(row_count, 2 * (5 * row_count * top_count // (8 * experts)))
    slot_table = expert_ids * capacity + slot_ids
    flat_index = slot_table.reshape(-1)
    token_number = jnp.broadcast_to(
        jnp.arange(row_count, dtype=jnp.int32)[:, None], (row_count, top_count)
    ).reshape(-1)
    slot_owner = jnp.zeros((experts * capacity,), jnp.int32).at[flat_index].set(token_number)
    send_x = jnp.take(tokens, slot_owner, axis=0).reshape(experts, capacity, feature_count)
    send_dy = jnp.take(cotangent, slot_owner, axis=0).reshape(experts, capacity, feature_count)
    full_gate, full_up, full_down = (
        lax.all_gather(s_gate, "exp", axis=0, tiled=True),
        lax.all_gather(s_up, "exp", axis=0, tiled=True),
        lax.all_gather(s_down, "exp", axis=0, tiled=True),
    )
    combined = jnp.zeros((row_count, feature_count), jnp.float32)
    arrived_x, arrived_dy = (
        lax.all_to_all(send_x, "exp", split_axis=0, concat_axis=0, tiled=True),
        lax.all_to_all(send_dy, "exp", split_axis=0, concat_axis=0, tiled=True),
    )
    pieces, part_gate = run_experts(arrived_x, arrived_dy, w_gate, w_up, w_down)
    returned, returned_gate = (
        lax.all_to_all(pieces, "exp", split_axis=0, concat_axis=0, tiled=True),
        lax.all_to_all(part_gate, "exp", split_axis=0, concat_axis=0, tiled=True),
    )
    flat_rows = returned.reshape(-1, feature_count)
    for column in range(top_count):
        picked = jnp.take(flat_rows, slot_table[:, column], axis=0)
        combined = combined + gates[:, column : column + 1] * picked.astype(jnp.float32)
    gate_part = (
        jnp.take(returned_gate.reshape(-1), flat_index)
        .reshape(row_count, top_count)
        .astype(jnp.float32)
    )
    gate_pre = jnp.dot(tokens, full_gate, preferred_element_type=jnp.float32)
    up_pre = jnp.dot(tokens, full_up, preferred_element_type=jnp.float32)
    grad_out = jnp.dot(cotangent, full_down, preferred_element_type=jnp.float32)
    grad_gate, grad_up, hidden = swiglu_grads(gate_pre, up_pre, grad_out)
    combined = combined + contract_back(grad_gate, full_gate) + contract_back(grad_up, full_up)
    dx_half, gate_half = (
        lax.psum_scatter(combined, "sp", scatter_dimension=1, tiled=True),
        lax.psum_scatter(gate_part, "sp", scatter_dimension=1, tiled=True),
    )
    return (dx_half.astype(jnp.bfloat16), gate_half)


def solution(mesh):
    in_specs = (
        P(("grp", "exp"), None),
        P(("grp", "exp"), None),
        P(("grp", "exp"), None),
        P(("grp", "exp"), None),
        P(("grp", "exp"), None),
        P("exp", None, "sp"),
        P("exp", None, "sp"),
        P("exp", None, "sp"),
        P("exp", "sp"),
        P("exp", "sp"),
        P("exp", "sp"),
    )
    out_specs = (P(("grp", "exp"), "sp"), P(("grp", "exp"), "sp"))
    fused = mesh.shape["grp"] == 2 and mesh.shape["sp"] == 2 and mesh.shape["exp"] == 8
    chosen = fused_body if fused else body
    return jax.shard_map(chosen, mesh=mesh, in_specs=in_specs, out_specs=out_specs, check_vma=False)
```

```python
import functools
import jax
import jax.numpy as jnp
from jax import lax
from jax.experimental import pallas as pl
from jax.experimental.pallas import tpu as pltpu
from jax.sharding import PartitionSpec as P

MESH = pl.DeviceIdType.MESH
LANE = 128
EAGER = 1


def ceil_lanes(count):
    return (count + LANE - 1) // LANE * LANE


def kernel(
    n, x_ref, dy_ref, ids_ref, gates_ref, wg_ref, wu_ref, wd_ref, sg_ref, su_ref, sd_ref,
    out_ref, gg_ref,
    tok, weights, shared_in, shared_ref, pair_out, pair_in, sum_out, sum_in,
    factor_out, factor_in, gate_out, gate_in,
    local_sem, tok_send, tok_recv, sib_send, sib_recv, pair_send, pair_recv,
    sum_send, sum_recv, w_send, w_recv, fw_send, fw_recv,
    factor_send, factor_recv, gate_send, gate_recv,
):
    rows, depth = x_ref.shape
    units = wg_ref.shape[2]
    top = ids_ref.shape[0]
    shared_rows = shared_ref.shape[1]
    share = sg_ref.shape[1] // n
    part_rows = shared_rows // 2
    swide = shared_ref.shape[2] // 3
    half = depth // 2
    half_rows = rows // 2
    x_wide = 2 * units + 2 * swide
    shared_at = 2 * units
    down_at = x_wide
    grp, exp, core = lax.axis_index("grp"), lax.axis_index("exp"), lax.axis_index("sp")
    other_grp, other_core = 1 - grp, 1 - core

    side, along = exp % 2, exp // 2
    place = (1 - side) * along + side * (n - 1 - along)

    def device_at(where):
        back = where // (n // 2)
        return (1 - back) * (2 * where) + back * (2 * (n - 1 - where) + 1)

    onward = (device_at((place + 1) % n), device_at((place + n - 1) % n))

    loads = [
        (x_ref, tok.at[0, 0]),
        (dy_ref, tok.at[0, 1]),
        (sg_ref, shared_in.at[0]),
        (su_ref, shared_in.at[1]),
        (sd_ref, shared_in.at[2]),
        (wg_ref.at[0], weights.at[:, pl.ds(0, units)]),
        (wu_ref.at[0], weights.at[:, pl.ds(units, units)]),
        (wd_ref.at[0], weights.at[:, pl.ds(down_at + swide, units)]),
    ]
    loads = [
        pltpu.make_async_copy(src, dst, local_sem.at[i]) for i, (src, dst) in enumerate(loads)
    ]
    for load in loads:
        load.start()

    barrier = pltpu.get_barrier_semaphore()
    for k in range(1, n):
        pl.semaphore_signal(
            barrier, inc=1, device_id={"exp": (exp + k) % n}, device_id_type=MESH
        )
    pl.semaphore_signal(barrier, inc=1, device_id={"sp": other_core}, device_id_type=MESH)
    pl.semaphore_signal(barrier, inc=1, device_id={"grp": other_grp}, device_id_type=MESH)

    row_lane = lax.broadcasted_iota(jnp.int32, (8, rows), 1)
    for i in range(n):
        factor = jnp.zeros((1, rows), jnp.float32)
        for k in range(top):
            factor = factor + jnp.where(ids_ref[k : k + 1, :] == i, gates_ref[k : k + 1, :], 0.0)
        factor_out[i] = jnp.broadcast_to(factor, (8, rows))
    factor_in[exp] = factor_out[exp]

    loads[0].wait()
    loads[1].wait()
    pl.semaphore_wait(barrier, n + 1)

    def token_copy(step, way):
        part = pl.ds(way * half_rows, half_rows)
        return pltpu.make_async_remote_copy(
            src_ref=tok.at[step, core, part],
            dst_ref=tok.at[step + 1, core, part],
            send_sem=tok_send.at[way, step],
            recv_sem=tok_recv.at[way, step + 1],
            device_id={"exp": onward[way]},
            device_id_type=MESH,
        )

    def token_arrival(step, way):
        part = pl.ds(way * half_rows, half_rows)
        return pltpu.make_async_remote_copy(
            src_ref=tok.at[step, core, part],
            dst_ref=tok.at[step, core, part],
            send_sem=tok_send.at[way, step],
            recv_sem=tok_recv.at[way, step],
            device_id={"exp": onward[way]},
            device_id_type=MESH,
        )

    def sibling_copy(step, which):
        return pltpu.make_async_remote_copy(
            src_ref=tok.at[step, which],
            dst_ref=tok.at[step, which],
            send_sem=sib_send.at[step],
            recv_sem=sib_recv.at[step],
            device_id={"sp": other_core},
            device_id_type=MESH,
        )

    def pair_copy(step):
        return pltpu.make_async_remote_copy(
            src_ref=pair_out.at[step],
            dst_ref=pair_in.at[step],
            send_sem=pair_send.at[step],
            recv_sem=pair_recv.at[step],
            device_id={"sp": other_core},
            device_id_type=MESH,
        )

    def sum_copy(step, way):
        part = pl.ds(way * half_rows, half_rows)
        return pltpu.make_async_remote_copy(
            src_ref=sum_out.at[step, part],
            dst_ref=sum_in.at[step, part],
            send_sem=sum_send.at[way, step],
            recv_sem=sum_recv.at[way, step],
            device_id={"exp": onward[way]},
            device_id_type=MESH,
        )

    def shared_block(owner, part):
        return weights.at[
            pl.ds(owner * shared_rows + part * part_rows, part_rows),
            pl.ds(shared_at, 3 * swide),
        ]

    def weight_copy(k):
        target = (exp + k) % n
        return pltpu.make_async_remote_copy(
            src_ref=shared_ref.at[target, pl.ds(grp * part_rows, part_rows)],
            dst_ref=shared_block(exp, grp),
            send_sem=w_send.at[k],
            recv_sem=w_recv.at[k],
            device_id={"exp": target},
            device_id_type=MESH,
        )

    def weight_arrival(k):
        block = shared_block((exp + n - k) % n, grp)
        return pltpu.make_async_remote_copy(
            src_ref=block,
            dst_ref=block,
            send_sem=w_send.at[k],
            recv_sem=w_recv.at[k],
            device_id={"exp": (exp + k) % n},
            device_id_type=MESH,
        )

    def weight_forward(k, part):
        block = shared_block((exp + n - k) % n, part)
        return pltpu.make_async_remote_copy(
            src_ref=block,
            dst_ref=block,
            send_sem=fw_send.at[k],
            recv_sem=fw_recv.at[k],
            device_id={"grp": other_grp},
            device_id_type=MESH,
        )

    def factor_copy(k):
        target = (exp + k) % n
        return pltpu.make_async_remote_copy(
            src_ref=factor_out.at[target],
            dst_ref=factor_in.at[exp],
            send_sem=factor_send.at[k],
            recv_sem=factor_recv.at[k],
            device_id={"exp": target},
            device_id_type=MESH,
        )

    def factor_arrival(k):
        return pltpu.make_async_remote_copy(
            src_ref=factor_out.at[(exp + k) % n],
            dst_ref=factor_in.at[(exp + n - k) % n],
            send_sem=factor_send.at[k],
            recv_sem=factor_recv.at[k],
            device_id={"exp": (exp + k) % n},
            device_id_type=MESH,
        )

    def behind(step, way):
        return device_at((place + n - step) % n if way == 0 else (place + step) % n)

    def gate_copy(step, way):
        return pltpu.make_async_remote_copy(
            src_ref=gate_out.at[step],
            dst_ref=gate_in.at[way, exp],
            send_sem=gate_send.at[way, step],
            recv_sem=gate_recv.at[way, step],
            device_id={"exp": behind(step, way)},
            device_id_type=MESH,
        )

    def gate_arrival(step, way):
        return pltpu.make_async_remote_copy(
            src_ref=gate_out.at[step],
            dst_ref=gate_in.at[way, behind(step, 1 - way)],
            send_sem=gate_send.at[way, step],
            recv_sem=gate_recv.at[way, step],
            device_id={"exp": behind(step, way)},
            device_id_type=MESH,
        )

    for way in range(2):
        token_copy(0, way).start()
    for k in range(1, n):
        factor_copy(k).start()
    for load in loads[2:5]:
        load.wait()
    for i in range(n):
        for j in range(3):
            piece = shared_in[j, :, i * share : (i + 1) * share]
            if swide > share:
                blank = jnp.zeros((shared_rows, swide - share), jnp.bfloat16)
                piece = jnp.concatenate([piece, blank], axis=1)
            shared_ref[i, :, pl.ds(j * swide, swide)] = piece
    for k in range(1, n):
        weight_copy(k).start()
    own_shared = pltpu.make_async_copy(
        shared_ref.at[exp],
        weights.at[pl.ds(exp * shared_rows, shared_rows), pl.ds(shared_at, 3 * swide)],
        local_sem.at[8],
    )
    own_shared.start()

    def back(grads, start, first_unit, unit_count):
        return lax.dot_general(
            grads,
            weights[pl.ds(start, half), pl.ds(first_unit, unit_count)],
            (((1,), (1,)), ((), ())),
            preferred_element_type=jnp.float32,
        )

    def grads_of(gate_pre, up_pre, grad_out):
        sigmoid_val = jax.nn.sigmoid(gate_pre)
        silu_val = gate_pre * sigmoid_val
        grad_gate = grad_out * up_pre * sigmoid_val * (1.0 + gate_pre * (1.0 - sigmoid_val))
        grad_up = grad_out * silu_val
        return (
            jnp.concatenate(
                [grad_gate.astype(jnp.bfloat16), grad_up.astype(jnp.bfloat16)], axis=1
            ),
            silu_val * up_pre,
        )

    def contribution(step):
        forward = jnp.dot(
            tok[step, 0],
            weights[:, pl.ds(0, x_wide)],
            preferred_element_type=jnp.float32,
        )
        down = jnp.dot(
            tok[step, 1],
            weights[:, pl.ds(down_at, swide + units)],
            preferred_element_type=jnp.float32,
        )
        grad_out = down[:, swide:]
        routed, hidden = grads_of(forward[:, :units], forward[:, units : 2 * units], grad_out)
        shared, unused = grads_of(
            forward[:, shared_at : shared_at + swide],
            forward[:, shared_at + swide :],
            down[:, :swide],
        )
        gate_part = jnp.sum(grad_out * hidden, axis=1, keepdims=True)
        gate_part = gate_part.astype(jnp.bfloat16).astype(jnp.float32)
        upper = factor_in[behind(step, 0)]
        lower = factor_in[behind(step, 1)]
        scale = jnp.where(row_lane < half_rows, upper, lower)
        scale = jnp.broadcast_to(scale[0:1], (rows, rows)).T[:, 0:1]

        def columns(start):
            return scale * back(routed, start, 0, 2 * units) + back(
                shared, start, shared_at, 2 * swide
            )

        extra = jnp.broadcast_to(gate_part, (rows, LANE))
        pair_out[step, :, pl.ds(0, half)] = columns(other_core * half)
        pair_out[step, :, pl.ds(half, LANE)] = extra
        pair_copy(step).start()
        return columns(core * half), extra

    wide = pl.ds(0, half)
    tail = pl.ds(half, LANE)

    def pass_on(step):
        for way in range(2):
            token_arrival(step, way).wait_recv()

        @pl.when(step < n - 1)
        def _():
            for way in range(2):
                token_copy(step, way).start()

        sibling_copy(step, core).start()

    def one_step(step, carry):
        @pl.when((step == 1) | (step > EAGER))
        def _():
            pass_on(step)

        @pl.when(step == 1)
        def _():
            for early in range(2, EAGER + 1):
                pass_on(early)
            for k in range(1, n):
                weight_arrival(k).wait_recv()
                weight_forward(k, grp).start()
            for load in loads[5:]:
                load.wait()
            own_shared.wait()
            for k in range(1, n):
                factor_arrival(k).wait_recv()
            for k in range(1, n):
                weight_forward(k, other_grp).wait_recv()

        sibling_copy(step, other_core).wait_recv()
        kept, extra = contribution(step)
        pair_copy(step).wait_recv()
        kept = kept + pair_in[step, :, wide]

        @pl.when(step == 1)
        def _():
            sum_out[step] = kept.astype(jnp.bfloat16)

        @pl.when(step > 1)
        def _():
            for way in range(2):
                sum_copy(step - 1, way).wait_recv()
            total = kept + sum_in[step - 1].astype(jnp.float32)
            sum_out[step] = total.astype(jnp.bfloat16)

        for way in range(2):
            sum_copy(step, way).start()
        gate_out[step] = (extra + pair_in[step, :, tail]).T[0:8]
        for way in range(2):
            gate_copy(step, way).start()
        return carry

    lax.fori_loop(1, n, one_step, 0)

    kept, extra = contribution(0)
    pair_copy(0).wait_recv()
    gate_own = (extra + pair_in[0, :, tail]).T[0:8]
    gate_in[0, exp] = gate_own
    gate_in[1, exp] = gate_own
    for step in range(1, n):
        for way in range(2):
            gate_arrival(step, way).wait_recv()
    for k in range(top // 2):
        wanted = jnp.where(
            core == 0, ids_ref[k : k + 1, :], ids_ref[k + top // 2 : k + top // 2 + 1, :]
        )
        total = jnp.zeros((1, rows), jnp.float32)
        for i in range(n):
            gate_row = jnp.where(row_lane < half_rows, gate_in[0, i], gate_in[1, i])[0:1]
            total = total + jnp.where(wanted == i, gate_row, 0.0)
        gg_ref[k : k + 1, :] = total
    kept = kept + pair_in[0, :, wide]
    for way in range(2):
        sum_copy(n - 1, way).wait_recv()
    out_ref[...] = (kept + sum_in[n - 1].astype(jnp.float32)).astype(jnp.bfloat16)

    for k in range(1, n):
        weight_copy(k).wait_send()
        weight_forward(k, grp).wait_send()
        factor_copy(k).wait_send()
    pair_copy(0).wait_send()
    for way in range(2):
        token_copy(0, way).wait_send()

    def drain(step, carry):
        @pl.when(step < n - 1)
        def _():
            for way in range(2):
                token_copy(step, way).wait_send()

        sibling_copy(step, core).wait_send()
        pair_copy(step).wait_send()
        for way in range(2):
            sum_copy(step, way).wait_send()
            gate_copy(step, way).wait_send()
        return carry

    lax.fori_loop(1, n, drain, 0)


def fused_body(
    tokens, cotangent, expert_ids, slot_ids, gates, w_gate, w_up, w_down, s_gate, s_up, s_down
):
    n = lax.axis_size("exp")
    rows, depth = tokens.shape
    units = w_gate.shape[2]
    top = expert_ids.shape[1]
    shared_rows, shared_units = s_gate.shape
    swide = ceil_lanes(shared_units // n)
    half = depth // 2
    anywhere = pl.BlockSpec(memory_space=pl.ANY)
    vmem = pl.BlockSpec(memory_space=pltpu.VMEM)
    dma = pltpu.SemaphoreType.DMA
    flops = 2 * n * rows * depth * 5 * (units + swide)
    input_grad, gate_grads = pl.pallas_call(
        functools.partial(kernel, n),
        out_shape=(
            jax.ShapeDtypeStruct((rows, half), jnp.bfloat16),
            jax.ShapeDtypeStruct((top // 2, rows), jnp.float32),
        ),
        in_specs=[anywhere, anywhere, vmem, vmem] + [anywhere] * 6,
        out_specs=(vmem, vmem),
        scratch_shapes=[
            pltpu.VMEM((n, 2, rows, depth), jnp.bfloat16),
            pltpu.VMEM((depth, 3 * units + 3 * swide), jnp.bfloat16),
            pltpu.VMEM((3, shared_rows, shared_units), jnp.bfloat16),
            pltpu.VMEM((n, shared_rows, 3 * swide), jnp.bfloat16),
            pltpu.VMEM((n, rows, half + LANE), jnp.float32),
            pltpu.VMEM((n, rows, half + LANE), jnp.float32),
            pltpu.VMEM((n, rows, half), jnp.bfloat16),
            pltpu.VMEM((n, rows, half), jnp.bfloat16),
            pltpu.VMEM((n, 8, rows), jnp.float32),
            pltpu.VMEM((n, 8, rows), jnp.float32),
            pltpu.VMEM((n, 8, rows), jnp.float32),
            pltpu.VMEM((2, n, 8, rows), jnp.float32),
            dma((9,)),
            dma((2, n)), dma((2, n)),
            dma((n,)), dma((n,)),
            dma((n,)), dma((n,)),
            dma((2, n)), dma((2, n)),
            dma((n,)), dma((n,)),
            dma((n,)), dma((n,)),
            dma((n,)), dma((n,)),
            dma((2, n)), dma((2, n)),
        ],
        compiler_params=pltpu.CompilerParams(
            collective_id=0, has_side_effects=True, vmem_limit_bytes=56 * 1024 * 1024
        ),
        cost_estimate=pl.CostEstimate(
            flops=flops, bytes_accessed=32 * 1024 * 1024, transcendentals=0
        ),
    )(tokens, cotangent, expert_ids.T, gates.T, w_gate, w_up, w_down, s_gate, s_up, s_down)
    return input_grad, gate_grads.T


def swiglu_grads(gate_pre, up_pre, grad_out):
    sigmoid_val = jax.nn.sigmoid(gate_pre)
    silu_val = gate_pre * sigmoid_val
    grad_gate = grad_out * up_pre * sigmoid_val * (1.0 + gate_pre * (1.0 - sigmoid_val))
    grad_up = grad_out * silu_val
    return (grad_gate.astype(jnp.bfloat16), grad_up.astype(jnp.bfloat16), silu_val * up_pre)


def contract_back(grads, weight):
    return lax.dot_general(
        grads, weight, (((1,), (1,)), ((), ())), preferred_element_type=jnp.float32
    )


def run_experts(arrived_x, arrived_dy, w_gate, w_up, w_down):
    local_count = w_gate.shape[0]
    slot_count = arrived_x.shape[1]
    source_count = arrived_x.shape[0] // local_count

    def regroup(values):
        shaped = values.reshape((source_count, local_count) + values.shape[1:])
        return jnp.swapaxes(shaped, 0, 1).reshape(
            (local_count, source_count * slot_count) + values.shape[2:]
        )

    def ungroup(values):
        shaped = values.reshape((local_count, source_count, slot_count) + values.shape[2:])
        return jnp.swapaxes(shaped, 0, 1).reshape(
            (source_count * local_count, slot_count) + values.shape[2:]
        )

    rows_x = regroup(arrived_x)
    rows_dy = regroup(arrived_dy)
    gate_pre = jnp.einsum("erd,edh->erh", rows_x, w_gate, preferred_element_type=jnp.float32)
    up_pre = jnp.einsum("erd,edh->erh", rows_x, w_up, preferred_element_type=jnp.float32)
    grad_out = jnp.einsum("erd,edh->erh", rows_dy, w_down, preferred_element_type=jnp.float32)
    grad_gate, grad_up, hidden = swiglu_grads(gate_pre, up_pre, grad_out)
    part_gate = jnp.sum(grad_out * hidden, axis=2).astype(jnp.bfloat16)
    both_grads = jnp.concatenate([grad_gate, grad_up], axis=2)
    both_weights = jnp.concatenate([w_gate, w_up], axis=2)
    pieces = jnp.einsum(
        "erh,edh->erd", both_grads, both_weights, preferred_element_type=jnp.float32
    )
    return (ungroup(pieces.astype(jnp.bfloat16)), ungroup(part_gate))


def body(
    tokens, cotangent, expert_ids, slot_ids, gates, w_gate, w_up, w_down, s_gate, s_up, s_down
):
    row_count, feature_count = tokens.shape
    top_count = expert_ids.shape[1]
    experts = w_gate.shape[0] * lax.axis_size("exp")
    capacity = min(row_count, 2 * (5 * row_count * top_count // (8 * experts)))
    slot_table = expert_ids * capacity + slot_ids
    flat_index = slot_table.reshape(-1)
    token_number = jnp.broadcast_to(
        jnp.arange(row_count, dtype=jnp.int32)[:, None], (row_count, top_count)
    ).reshape(-1)
    slot_owner = jnp.zeros((experts * capacity,), jnp.int32).at[flat_index].set(token_number)
    send_x = jnp.take(tokens, slot_owner, axis=0).reshape(experts, capacity, feature_count)
    send_dy = jnp.take(cotangent, slot_owner, axis=0).reshape(experts, capacity, feature_count)
    full_gate, full_up, full_down = (
        lax.all_gather(s_gate, "exp", axis=0, tiled=True),
        lax.all_gather(s_up, "exp", axis=0, tiled=True),
        lax.all_gather(s_down, "exp", axis=0, tiled=True),
    )
    combined = jnp.zeros((row_count, feature_count), jnp.float32)
    arrived_x, arrived_dy = (
        lax.all_to_all(send_x, "exp", split_axis=0, concat_axis=0, tiled=True),
        lax.all_to_all(send_dy, "exp", split_axis=0, concat_axis=0, tiled=True),
    )
    pieces, part_gate = run_experts(arrived_x, arrived_dy, w_gate, w_up, w_down)
    returned, returned_gate = (
        lax.all_to_all(pieces, "exp", split_axis=0, concat_axis=0, tiled=True),
        lax.all_to_all(part_gate, "exp", split_axis=0, concat_axis=0, tiled=True),
    )
    flat_rows = returned.reshape(-1, feature_count)
    for column in range(top_count):
        picked = jnp.take(flat_rows, slot_table[:, column], axis=0)
        combined = combined + gates[:, column : column + 1] * picked.astype(jnp.float32)
    gate_part = (
        jnp.take(returned_gate.reshape(-1), flat_index)
        .reshape(row_count, top_count)
        .astype(jnp.float32)
    )
    gate_pre = jnp.dot(tokens, full_gate, preferred_element_type=jnp.float32)
    up_pre = jnp.dot(tokens, full_up, preferred_element_type=jnp.float32)
    grad_out = jnp.dot(cotangent, full_down, preferred_element_type=jnp.float32)
    grad_gate, grad_up, hidden = swiglu_grads(gate_pre, up_pre, grad_out)
    combined = combined + contract_back(grad_gate, full_gate) + contract_back(grad_up, full_up)
    dx_half, gate_half = (
        lax.psum_scatter(combined, "sp", scatter_dimension=1, tiled=True),
        lax.psum_scatter(gate_part, "sp", scatter_dimension=1, tiled=True),
    )
    return (dx_half.astype(jnp.bfloat16), gate_half)


def solution(mesh):
    in_specs = (
        P(("grp", "exp"), None),
        P(("grp", "exp"), None),
        P(("grp", "exp"), None),
        P(("grp", "exp"), None),
        P(("grp", "exp"), None),
        P("exp", None, "sp"),
        P("exp", None, "sp"),
        P("exp", None, "sp"),
        P("exp", "sp"),
        P("exp", "sp"),
        P("exp", "sp"),
    )
    out_specs = (P(("grp", "exp"), "sp"), P(("grp", "exp"), "sp"))
    fused = mesh.shape["grp"] == 2 and mesh.shape["sp"] == 2 and mesh.shape["exp"] == 8
    chosen = fused_body if fused else body
    return jax.shard_map(chosen, mesh=mesh, in_specs=in_specs, out_specs=out_specs, check_vma=False)
```

```python
import functools
import jax
import jax.numpy as jnp
from jax import lax
from jax.experimental import pallas as pl
from jax.experimental.pallas import tpu as pltpu
from jax.sharding import PartitionSpec as P

MESH = pl.DeviceIdType.MESH
LANE = 128


def ceil_lanes(count):
    return (count + LANE - 1) // LANE * LANE


def kernel(
    n, x_ref, dy_ref, ids_ref, gates_ref, wg_ref, wu_ref, wd_ref, sg_ref, su_ref, sd_ref,
    out_ref, gg_ref,
    kept_buf, tok, weights, shared_in, shared_ref, pair_out, pair_in, sum_out, sum_in,
    factor_out, factor_in, gate_out, gate_in,
    local_sem, tok_send, tok_recv, sib_send, sib_recv, pair_send, pair_recv,
    sum_send, sum_recv, w_send, w_recv, fw_send, fw_recv,
    factor_send, factor_recv, gate_send, gate_recv,
):
    rows, depth = x_ref.shape
    units = wg_ref.shape[2]
    top = ids_ref.shape[0]
    shared_rows = shared_ref.shape[1]
    share = sg_ref.shape[1] // n
    part_rows = shared_rows // 2
    swide = shared_ref.shape[2] // 3
    half = depth // 2
    half_rows = rows // 2
    x_wide = 2 * units + 2 * swide
    shared_at = 2 * units
    down_at = x_wide
    grp, exp, core = lax.axis_index("grp"), lax.axis_index("exp"), lax.axis_index("sp")
    other_grp, other_core = 1 - grp, 1 - core

    side, along = exp % 2, exp // 2
    place = (1 - side) * along + side * (n - 1 - along)

    def device_at(where):
        back = where // (n // 2)
        return (1 - back) * (2 * where) + back * (2 * (n - 1 - where) + 1)

    onward = (device_at((place + 1) % n), device_at((place + n - 1) % n))

    loads = [
        (x_ref, tok.at[0, 0]),
        (dy_ref, tok.at[0, 1]),
        (sg_ref, shared_in.at[0]),
        (su_ref, shared_in.at[1]),
        (sd_ref, shared_in.at[2]),
        (wg_ref.at[0], weights.at[:, pl.ds(0, units)]),
        (wu_ref.at[0], weights.at[:, pl.ds(units, units)]),
        (wd_ref.at[0], weights.at[:, pl.ds(down_at + swide, units)]),
    ]
    loads = [
        pltpu.make_async_copy(src, dst, local_sem.at[i]) for i, (src, dst) in enumerate(loads)
    ]
    for load in loads:
        load.start()

    barrier = pltpu.get_barrier_semaphore()
    for k in range(1, n):
        pl.semaphore_signal(
            barrier, inc=1, device_id={"exp": (exp + k) % n}, device_id_type=MESH
        )
    pl.semaphore_signal(barrier, inc=1, device_id={"sp": other_core}, device_id_type=MESH)
    pl.semaphore_signal(barrier, inc=1, device_id={"grp": other_grp}, device_id_type=MESH)

    row_lane = lax.broadcasted_iota(jnp.int32, (8, rows), 1)
    for i in range(n):
        factor = jnp.zeros((1, rows), jnp.float32)
        for k in range(top):
            factor = factor + jnp.where(ids_ref[k : k + 1, :] == i, gates_ref[k : k + 1, :], 0.0)
        factor_out[i] = jnp.broadcast_to(factor, (8, rows))
    factor_in[exp] = factor_out[exp]

    loads[0].wait()
    loads[1].wait()
    pl.semaphore_wait(barrier, n + 1)

    def token_copy(step, way):
        part = pl.ds(way * half_rows, half_rows)
        return pltpu.make_async_remote_copy(
            src_ref=tok.at[step, core, part],
            dst_ref=tok.at[step + 1, core, part],
            send_sem=tok_send.at[way, step],
            recv_sem=tok_recv.at[way, step + 1],
            device_id={"exp": onward[way]},
            device_id_type=MESH,
        )

    def token_arrival(step, way):
        part = pl.ds(way * half_rows, half_rows)
        return pltpu.make_async_remote_copy(
            src_ref=tok.at[step, core, part],
            dst_ref=tok.at[step, core, part],
            send_sem=tok_send.at[way, step],
            recv_sem=tok_recv.at[way, step],
            device_id={"exp": onward[way]},
            device_id_type=MESH,
        )

    def sibling_copy(step, which):
        return pltpu.make_async_remote_copy(
            src_ref=tok.at[step, which],
            dst_ref=tok.at[step, which],
            send_sem=sib_send.at[step],
            recv_sem=sib_recv.at[step],
            device_id={"sp": other_core},
            device_id_type=MESH,
        )

    def pair_copy(step):
        return pltpu.make_async_remote_copy(
            src_ref=pair_out.at[step],
            dst_ref=pair_in.at[step],
            send_sem=pair_send.at[step],
            recv_sem=pair_recv.at[step],
            device_id={"sp": other_core},
            device_id_type=MESH,
        )

    def sum_copy(step, way):
        part = pl.ds(way * half_rows, half_rows)
        return pltpu.make_async_remote_copy(
            src_ref=sum_out.at[step, part],
            dst_ref=sum_in.at[step, part],
            send_sem=sum_send.at[way, step],
            recv_sem=sum_recv.at[way, step],
            device_id={"exp": onward[way]},
            device_id_type=MESH,
        )

    def shared_block(owner, part):
        return weights.at[
            pl.ds(owner * shared_rows + part * part_rows, part_rows),
            pl.ds(shared_at, 3 * swide),
        ]

    def weight_copy(k):
        target = (exp + k) % n
        return pltpu.make_async_remote_copy(
            src_ref=shared_ref.at[target, pl.ds(grp * part_rows, part_rows)],
            dst_ref=shared_block(exp, grp),
            send_sem=w_send.at[k],
            recv_sem=w_recv.at[k],
            device_id={"exp": target},
            device_id_type=MESH,
        )

    def weight_arrival(k):
        block = shared_block((exp + n - k) % n, grp)
        return pltpu.make_async_remote_copy(
            src_ref=block,
            dst_ref=block,
            send_sem=w_send.at[k],
            recv_sem=w_recv.at[k],
            device_id={"exp": (exp + k) % n},
            device_id_type=MESH,
        )

    def weight_forward(k, part):
        block = shared_block((exp + n - k) % n, part)
        return pltpu.make_async_remote_copy(
            src_ref=block,
            dst_ref=block,
            send_sem=fw_send.at[k],
            recv_sem=fw_recv.at[k],
            device_id={"grp": other_grp},
            device_id_type=MESH,
        )

    def factor_copy(k):
        target = (exp + k) % n
        return pltpu.make_async_remote_copy(
            src_ref=factor_out.at[target],
            dst_ref=factor_in.at[exp],
            send_sem=factor_send.at[k],
            recv_sem=factor_recv.at[k],
            device_id={"exp": target},
            device_id_type=MESH,
        )

    def factor_arrival(k):
        return pltpu.make_async_remote_copy(
            src_ref=factor_out.at[(exp + k) % n],
            dst_ref=factor_in.at[(exp + n - k) % n],
            send_sem=factor_send.at[k],
            recv_sem=factor_recv.at[k],
            device_id={"exp": (exp + k) % n},
            device_id_type=MESH,
        )

    def behind(step, way):
        return device_at((place + n - step) % n if way == 0 else (place + step) % n)

    def gate_copy(step, way):
        return pltpu.make_async_remote_copy(
            src_ref=gate_out.at[step],
            dst_ref=gate_in.at[way, exp],
            send_sem=gate_send.at[way, step],
            recv_sem=gate_recv.at[way, step],
            device_id={"exp": behind(step, way)},
            device_id_type=MESH,
        )

    def gate_arrival(step, way):
        return pltpu.make_async_remote_copy(
            src_ref=gate_out.at[step],
            dst_ref=gate_in.at[way, behind(step, 1 - way)],
            send_sem=gate_send.at[way, step],
            recv_sem=gate_recv.at[way, step],
            device_id={"exp": behind(step, way)},
            device_id_type=MESH,
        )

    for way in range(2):
        token_copy(0, way).start()
    for k in range(1, n):
        factor_copy(k).start()
    for load in loads[2:5]:
        load.wait()
    for i in range(n):
        for j in range(3):
            piece = shared_in[j, :, i * share : (i + 1) * share]
            if swide > share:
                blank = jnp.zeros((shared_rows, swide - share), jnp.bfloat16)
                piece = jnp.concatenate([piece, blank], axis=1)
            shared_ref[i, :, pl.ds(j * swide, swide)] = piece
    for k in range(1, n):
        weight_copy(k).start()
    own_shared = pltpu.make_async_copy(
        shared_ref.at[exp],
        weights.at[pl.ds(exp * shared_rows, shared_rows), pl.ds(shared_at, 3 * swide)],
        local_sem.at[8],
    )
    own_shared.start()

    def back(grads, start, first_unit, unit_count):
        return lax.dot_general(
            grads,
            weights[pl.ds(start, half), pl.ds(first_unit, unit_count)],
            (((1,), (1,)), ((), ())),
            preferred_element_type=jnp.float32,
        )

    def grads_of(gate_pre, up_pre, grad_out):
        sigmoid_val = jax.nn.sigmoid(gate_pre)
        silu_val = gate_pre * sigmoid_val
        grad_gate = grad_out * up_pre * sigmoid_val * (1.0 + gate_pre * (1.0 - sigmoid_val))
        grad_up = grad_out * silu_val
        return (
            jnp.concatenate(
                [grad_gate.astype(jnp.bfloat16), grad_up.astype(jnp.bfloat16)], axis=1
            ),
            silu_val * up_pre,
        )

    def contribution(step):
        forward = jnp.dot(
            tok[step, 0],
            weights[:, pl.ds(0, x_wide)],
            preferred_element_type=jnp.float32,
        )
        down = jnp.dot(
            tok[step, 1],
            weights[:, pl.ds(down_at, swide + units)],
            preferred_element_type=jnp.float32,
        )
        grad_out = down[:, swide:]
        routed, hidden = grads_of(forward[:, :units], forward[:, units : 2 * units], grad_out)
        shared, unused = grads_of(
            forward[:, shared_at : shared_at + swide],
            forward[:, shared_at + swide :],
            down[:, :swide],
        )
        gate_part = jnp.sum(grad_out * hidden, axis=1, keepdims=True)
        gate_part = gate_part.astype(jnp.bfloat16).astype(jnp.float32)
        upper = factor_in[behind(step, 0)]
        lower = factor_in[behind(step, 1)]
        scale = jnp.where(row_lane < half_rows, upper, lower)
        scale = jnp.broadcast_to(scale[0:1], (rows, rows)).T[:, 0:1]

        def columns(start):
            return scale * back(routed, start, 0, 2 * units) + back(
                shared, start, shared_at, 2 * swide
            )

        extra = jnp.broadcast_to(gate_part, (rows, LANE))
        pair_out[step, :, pl.ds(0, half)] = columns(other_core * half)
        pair_out[step, :, pl.ds(half, LANE)] = extra
        pair_copy(step).start()
        return columns(core * half), extra

    wide = pl.ds(0, half)
    tail = pl.ds(half, LANE)

    def pass_on(step):
        for way in range(2):
            token_arrival(step, way).wait_recv()

        @pl.when(step < n - 1)
        def _():
            for way in range(2):
                token_copy(step, way).start()

        sibling_copy(step, core).start()

    def prepare(step):
        kept, extra = contribution(step)
        kept_buf[step % 2, :, wide] = kept
        kept_buf[step % 2, :, tail] = extra

    def finish(step):
        pair_copy(step).wait_recv()
        kept = kept_buf[step % 2, :, wide] + pair_in[step, :, wide]

        @pl.when(step == 1)
        def _():
            sum_out[step] = kept.astype(jnp.bfloat16)

        @pl.when(step > 1)
        def _():
            for way in range(2):
                sum_copy(step - 1, way).wait_recv()
            total = kept + sum_in[step - 1].astype(jnp.float32)
            sum_out[step] = total.astype(jnp.bfloat16)

        for way in range(2):
            sum_copy(step, way).start()
        extra = kept_buf[step % 2, :, tail] + pair_in[step, :, tail]
        gate_out[step] = extra.T[0:8]
        for way in range(2):
            gate_copy(step, way).start()

    def one_step(step, carry):
        @pl.when(step < n - 1)
        def _():
            pass_on(step + 1)

        finish(step)

        @pl.when(step < n - 1)
        def _():
            sibling_copy(step + 1, other_core).wait_recv()

        prepare((step + 1) % n)
        return carry

    pass_on(1)
    for k in range(1, n):
        weight_arrival(k).wait_recv()
        weight_forward(k, grp).start()
    for load in loads[5:]:
        load.wait()
    own_shared.wait()
    for k in range(1, n):
        factor_arrival(k).wait_recv()
    for k in range(1, n):
        weight_forward(k, other_grp).wait_recv()
    sibling_copy(1, other_core).wait_recv()
    prepare(1)
    lax.fori_loop(1, n, one_step, 0)
    pair_copy(0).wait_recv()
    kept = kept_buf[0, :, wide]
    extra = kept_buf[0, :, tail]
    gate_own = (extra + pair_in[0, :, tail]).T[0:8]
    gate_in[0, exp] = gate_own
    gate_in[1, exp] = gate_own
    for step in range(1, n):
        for way in range(2):
            gate_arrival(step, way).wait_recv()
    for k in range(top // 2):
        wanted = jnp.where(
            core == 0, ids_ref[k : k + 1, :], ids_ref[k + top // 2 : k + top // 2 + 1, :]
        )
        total = jnp.zeros((1, rows), jnp.float32)
        for i in range(n):
            gate_row = jnp.where(row_lane < half_rows, gate_in[0, i], gate_in[1, i])[0:1]
            total = total + jnp.where(wanted == i, gate_row, 0.0)
        gg_ref[k : k + 1, :] = total
    kept = kept + pair_in[0, :, wide]
    for way in range(2):
        sum_copy(n - 1, way).wait_recv()
    out_ref[...] = (kept + sum_in[n - 1].astype(jnp.float32)).astype(jnp.bfloat16)

    for k in range(1, n):
        weight_copy(k).wait_send()
        weight_forward(k, grp).wait_send()
        factor_copy(k).wait_send()
    pair_copy(0).wait_send()
    for way in range(2):
        token_copy(0, way).wait_send()

    def drain(step, carry):
        @pl.when(step < n - 1)
        def _():
            for way in range(2):
                token_copy(step, way).wait_send()

        sibling_copy(step, core).wait_send()
        pair_copy(step).wait_send()
        for way in range(2):
            sum_copy(step, way).wait_send()
            gate_copy(step, way).wait_send()
        return carry

    lax.fori_loop(1, n, drain, 0)


def fused_body(
    tokens, cotangent, expert_ids, slot_ids, gates, w_gate, w_up, w_down, s_gate, s_up, s_down
):
    n = lax.axis_size("exp")
    rows, depth = tokens.shape
    units = w_gate.shape[2]
    top = expert_ids.shape[1]
    shared_rows, shared_units = s_gate.shape
    swide = ceil_lanes(shared_units // n)
    half = depth // 2
    anywhere = pl.BlockSpec(memory_space=pl.ANY)
    vmem = pl.BlockSpec(memory_space=pltpu.VMEM)
    dma = pltpu.SemaphoreType.DMA
    flops = 2 * n * rows * depth * 5 * (units + swide)
    input_grad, gate_grads = pl.pallas_call(
        functools.partial(kernel, n),
        out_shape=(
            jax.ShapeDtypeStruct((rows, half), jnp.bfloat16),
            jax.ShapeDtypeStruct((top // 2, rows), jnp.float32),
        ),
        in_specs=[anywhere, anywhere, vmem, vmem] + [anywhere] * 6,
        out_specs=(vmem, vmem),
        scratch_shapes=[
            pltpu.VMEM((2, rows, half + LANE), jnp.float32),
            pltpu.VMEM((n, 2, rows, depth), jnp.bfloat16),
            pltpu.VMEM((depth, 3 * units + 3 * swide), jnp.bfloat16),
            pltpu.VMEM((3, shared_rows, shared_units), jnp.bfloat16),
            pltpu.VMEM((n, shared_rows, 3 * swide), jnp.bfloat16),
            pltpu.VMEM((n, rows, half + LANE), jnp.float32),
            pltpu.VMEM((n, rows, half + LANE), jnp.float32),
            pltpu.VMEM((n, rows, half), jnp.bfloat16),
            pltpu.VMEM((n, rows, half), jnp.bfloat16),
            pltpu.VMEM((n, 8, rows), jnp.float32),
            pltpu.VMEM((n, 8, rows), jnp.float32),
            pltpu.VMEM((n, 8, rows), jnp.float32),
            pltpu.VMEM((2, n, 8, rows), jnp.float32),
            dma((9,)),
            dma((2, n)), dma((2, n)),
            dma((n,)), dma((n,)),
            dma((n,)), dma((n,)),
            dma((2, n)), dma((2, n)),
            dma((n,)), dma((n,)),
            dma((n,)), dma((n,)),
            dma((n,)), dma((n,)),
            dma((2, n)), dma((2, n)),
        ],
        compiler_params=pltpu.CompilerParams(
            collective_id=0, has_side_effects=True, vmem_limit_bytes=56 * 1024 * 1024
        ),
        cost_estimate=pl.CostEstimate(
            flops=flops, bytes_accessed=32 * 1024 * 1024, transcendentals=0
        ),
    )(tokens, cotangent, expert_ids.T, gates.T, w_gate, w_up, w_down, s_gate, s_up, s_down)
    return input_grad, gate_grads.T


def swiglu_grads(gate_pre, up_pre, grad_out):
    sigmoid_val = jax.nn.sigmoid(gate_pre)
    silu_val = gate_pre * sigmoid_val
    grad_gate = grad_out * up_pre * sigmoid_val * (1.0 + gate_pre * (1.0 - sigmoid_val))
    grad_up = grad_out * silu_val
    return (grad_gate.astype(jnp.bfloat16), grad_up.astype(jnp.bfloat16), silu_val * up_pre)


def contract_back(grads, weight):
    return lax.dot_general(
        grads, weight, (((1,), (1,)), ((), ())), preferred_element_type=jnp.float32
    )


def run_experts(arrived_x, arrived_dy, w_gate, w_up, w_down):
    local_count = w_gate.shape[0]
    slot_count = arrived_x.shape[1]
    source_count = arrived_x.shape[0] // local_count

    def regroup(values):
        shaped = values.reshape((source_count, local_count) + values.shape[1:])
        return jnp.swapaxes(shaped, 0, 1).reshape(
            (local_count, source_count * slot_count) + values.shape[2:]
        )

    def ungroup(values):
        shaped = values.reshape((local_count, source_count, slot_count) + values.shape[2:])
        return jnp.swapaxes(shaped, 0, 1).reshape(
            (source_count * local_count, slot_count) + values.shape[2:]
        )

    rows_x = regroup(arrived_x)
    rows_dy = regroup(arrived_dy)
    gate_pre = jnp.einsum("erd,edh->erh", rows_x, w_gate, preferred_element_type=jnp.float32)
    up_pre = jnp.einsum("erd,edh->erh", rows_x, w_up, preferred_element_type=jnp.float32)
    grad_out = jnp.einsum("erd,edh->erh", rows_dy, w_down, preferred_element_type=jnp.float32)
    grad_gate, grad_up, hidden = swiglu_grads(gate_pre, up_pre, grad_out)
    part_gate = jnp.sum(grad_out * hidden, axis=2).astype(jnp.bfloat16)
    both_grads = jnp.concatenate([grad_gate, grad_up], axis=2)
    both_weights = jnp.concatenate([w_gate, w_up], axis=2)
    pieces = jnp.einsum(
        "erh,edh->erd", both_grads, both_weights, preferred_element_type=jnp.float32
    )
    return (ungroup(pieces.astype(jnp.bfloat16)), ungroup(part_gate))


def body(
    tokens, cotangent, expert_ids, slot_ids, gates, w_gate, w_up, w_down, s_gate, s_up, s_down
):
    row_count, feature_count = tokens.shape
    top_count = expert_ids.shape[1]
    experts = w_gate.shape[0] * lax.axis_size("exp")
    capacity = min(row_count, 2 * (5 * row_count * top_count // (8 * experts)))
    slot_table = expert_ids * capacity + slot_ids
    flat_index = slot_table.reshape(-1)
    token_number = jnp.broadcast_to(
        jnp.arange(row_count, dtype=jnp.int32)[:, None], (row_count, top_count)
    ).reshape(-1)
    slot_owner = jnp.zeros((experts * capacity,), jnp.int32).at[flat_index].set(token_number)
    send_x = jnp.take(tokens, slot_owner, axis=0).reshape(experts, capacity, feature_count)
    send_dy = jnp.take(cotangent, slot_owner, axis=0).reshape(experts, capacity, feature_count)
    full_gate, full_up, full_down = (
        lax.all_gather(s_gate, "exp", axis=0, tiled=True),
        lax.all_gather(s_up, "exp", axis=0, tiled=True),
        lax.all_gather(s_down, "exp", axis=0, tiled=True),
    )
    combined = jnp.zeros((row_count, feature_count), jnp.float32)
    arrived_x, arrived_dy = (
        lax.all_to_all(send_x, "exp", split_axis=0, concat_axis=0, tiled=True),
        lax.all_to_all(send_dy, "exp", split_axis=0, concat_axis=0, tiled=True),
    )
    pieces, part_gate = run_experts(arrived_x, arrived_dy, w_gate, w_up, w_down)
    returned, returned_gate = (
        lax.all_to_all(pieces, "exp", split_axis=0, concat_axis=0, tiled=True),
        lax.all_to_all(part_gate, "exp", split_axis=0, concat_axis=0, tiled=True),
    )
    flat_rows = returned.reshape(-1, feature_count)
    for column in range(top_count):
        picked = jnp.take(flat_rows, slot_table[:, column], axis=0)
        combined = combined + gates[:, column : column + 1] * picked.astype(jnp.float32)
    gate_part = (
        jnp.take(returned_gate.reshape(-1), flat_index)
        .reshape(row_count, top_count)
        .astype(jnp.float32)
    )
    gate_pre = jnp.dot(tokens, full_gate, preferred_element_type=jnp.float32)
    up_pre = jnp.dot(tokens, full_up, preferred_element_type=jnp.float32)
    grad_out = jnp.dot(cotangent, full_down, preferred_element_type=jnp.float32)
    grad_gate, grad_up, hidden = swiglu_grads(gate_pre, up_pre, grad_out)
    combined = combined + contract_back(grad_gate, full_gate) + contract_back(grad_up, full_up)
    dx_half, gate_half = (
        lax.psum_scatter(combined, "sp", scatter_dimension=1, tiled=True),
        lax.psum_scatter(gate_part, "sp", scatter_dimension=1, tiled=True),
    )
    return (dx_half.astype(jnp.bfloat16), gate_half)


def solution(mesh):
    in_specs = (
        P(("grp", "exp"), None),
        P(("grp", "exp"), None),
        P(("grp", "exp"), None),
        P(("grp", "exp"), None),
        P(("grp", "exp"), None),
        P("exp", None, "sp"),
        P("exp", None, "sp"),
        P("exp", None, "sp"),
        P("exp", "sp"),
        P("exp", "sp"),
        P("exp", "sp"),
    )
    out_specs = (P(("grp", "exp"), "sp"), P(("grp", "exp"), "sp"))
    fused = mesh.shape["grp"] == 2 and mesh.shape["sp"] == 2 and mesh.shape["exp"] == 8
    chosen = fused_body if fused else body
    return jax.shard_map(chosen, mesh=mesh, in_specs=in_specs, out_specs=out_specs, check_vma=False)
```
